32 devices in a mesh: strips: 2 (over y), wave: 4 (over x, core), cols: 4 (over z).
Axes of the slice: x: 2, y: 2, z: 4, core: 2. Of those that a mesh axis runs over, the one named last changes fastest.
Arguments:
- frames: bfloat16 [1024, 32, 4096], P('wave', 'strips', 'cols'), parts along dimension 1, may hold values from -6 to 6
- wavenumbers: float32 [1024], replicated, may hold values from 0 to 1
- band_start: int32 [6], replicated, may hold values from 0 to 384
- aperture_offset: int32 [64], P(('strips', 'cols')), parts along dimension 0, may hold values from 0 to 15
- aperture_count: int32 [64], P(('strips', 'cols')), parts along dimension 0, may hold values from 4 to 16
- reference_pixels: int32 [512], P('strips'), parts along dimension 0, may hold values from 0 to 65535, as said below
Outputs:
- cavity_maps: bfloat16 [6, 2, 128, 32, 4096], P(None, None, None, ('strips', 'wave'), 'cols'), parts along dimension 3
The draws below stay inside these ranges and needn't reach their ends.
There are 2 independent parts, one for each index of `strips`. The reference program is written for one: setup_inputs(seed, part) draws one part's arguments, and reference() takes and returns one part's arrays. A program takes and returns all parts, laid end to end along the dimension named above; an argument that names none is the same for every part. Nothing has to cross between parts.
Inputs may be any that keep to these rules, and one draw needn't show every extreme that they name: `reference_pixels`: the indices are distinct.
All inputs are finite; a program needn't handle non-finite values.
Results may differ from the reference program's by a relative error of at most 0.0056.
Values may be sent and summed in bfloat16 or wider, within the bound.
A program may use at most 128 MiB of HBM per device.

```python
import math
import jax
import jax.numpy as jnp
from jax import lax

F = 1024
ROWS = 16
COLBLK = 128
CAV = 6
NB = 128
REFN = 256
W = 4096
NCB = 32


def draw_reference_pixels(key, part):
    return jax.random.permutation(key, ROWS * W)[:REFN].astype(jnp.int32)


def set_ends(array, stream_key, least, top_value):
    index_at = [jax.random.randint(jax.random.fold_in(stream_key, axis), (), 0, length) for axis, length in enumerate(array.shape)]
    main_axis = array.shape.index(max(array.shape))
    neighbour = index_at[:main_axis] + [(index_at[main_axis] + 1) % array.shape[main_axis]] + index_at[main_axis + 1:]
    return array.at[tuple(index_at)].set(least).at[tuple(neighbour)].set(top_value)


def level_of(own_key, extent, shards, low, largest):
    def one(position, shards_of):
        draws = jax.random.uniform(jax.random.fold_in(jax.random.fold_in(own_key, 6), position), (shards_of,), jnp.float32, low / len(shards), largest / len(shards))
        return jnp.repeat(jnp.exp(draws), extent[position] // shards_of).reshape((-1,) + (1,) * (len(extent) - position - 1))

    level = one(*shards[0])
    for cut in shards[1:]:
        level = level * one(*cut)
    return level


def scatter_about(stream_key, dims, spread, most, shards=(), kind=jnp.bfloat16):
    result = jax.random.normal(stream_key, dims, jnp.float32) * spread
    if len(shards) > 0:
        result = level_of(stream_key, dims, shards, -0.22, 0.18) * result
    return jnp.clip(result, min=-most, max=most).astype(kind)


def setup_inputs(seed: int = 0, part: int = 0) -> dict:
    key_list = jax.random.split(jax.random.key(seed), 7)
    part_splits = jax.random.split(jax.random.fold_in(key_list[6], part), 7)
    return {
        "frames": scatter_about(part_splits[0], (F, ROWS, W), 1.0, 6.0, ((0, 4), (2, 4))),
        "wavenumbers": jnp.clip(jax.random.uniform(key_list[1], (F,), jnp.float32, 0.0, 1.0), 0.0, 1.0),
        "band_start": set_ends(jax.random.randint(key_list[2], (CAV,), 0, F // 2 - NB + 1), jax.random.fold_in(key_list[2], 1), 0, (F // 2 - NB + 1) - 1).astype(jnp.int32),
        "aperture_offset": set_ends(jax.random.randint(part_splits[3], (NCB,), 0, ROWS), jax.random.fold_in(part_splits[3], 1), 0, ROWS - 1).astype(jnp.int32),
        "aperture_count": set_ends(jax.random.randint(part_splits[4], (NCB,), 4, ROWS + 1), jax.random.fold_in(part_splits[4], 1), 4, ROWS).astype(jnp.int32),
        "reference_pixels": draw_reference_pixels(jax.random.fold_in(jax.random.fold_in(key_list[6], part), 71), part),
    }


TWO_PI = 2.0 * math.pi
EPS = 1e-06

def table_block(wavenumbers, band_start, first_row, count, bins_band, frame_total):
    rows = first_row + jnp.arange(count, dtype=jnp.int32)
    cavity = rows // (2 * bins_band)
    imag_part = rows // bins_band % 2
    offset_bin = rows % bins_band
    cav_ids = jnp.arange(band_start.shape[0], dtype=jnp.int32)
    start_of = lax.optimization_barrier(jnp.sum(jnp.where(cavity[:, None] == cav_ids[None, :], band_start[None, :], 0), axis=1))
    bins = (start_of + offset_bin).astype(jnp.float32)
    frame_pos = jnp.arange(frame_total, dtype=jnp.float32)
    window = (0.5 - 0.5 * jnp.cos(TWO_PI * (frame_pos + 0.5) / frame_total)) / math.sqrt(frame_total)
    angle_mat = bins[:, None] * wavenumbers[None, :] * TWO_PI
    value = jnp.where(imag_part[:, None] == 0, jnp.cos(angle_mat), -jnp.sin(angle_mat)) * window[None, :]
    return value.astype(jnp.bfloat16)

def reference(frames, wavenumbers, band_start, aperture_offset, aperture_count, reference_pixels):
    blocks = lax.map(lambda c: table_block(wavenumbers, band_start, c * 2 * NB, 2 * NB, NB, F), jnp.arange(CAV, dtype=jnp.int32))
    table = blocks.reshape(2 * CAV * NB, F)
    col_block = jnp.arange(W, dtype=jnp.int32) // COLBLK
    off_cols = aperture_offset[col_block]
    cnt_cols = aperture_count[col_block]
    row_ids = jnp.arange(ROWS, dtype=jnp.int32)[:, None]
    valid = ((row_ids >= off_cols[None, :]) & (row_ids < off_cols[None, :] + cnt_cols[None, :])).astype(jnp.bfloat16)
    flat_frames = frames.reshape(F, ROWS * W)
    flat_valid = valid.reshape(ROWS * W)
    ref_frames = flat_frames[:, reference_pixels] * flat_valid[reference_pixels][None, :]
    ref_spec = jnp.dot(table, ref_frames, preferred_element_type=jnp.float32).reshape(CAV, 2, NB, REFN)
    middle = ref_spec[:, :, NB // 2, :]
    ref_re = lax.optimization_barrier(jnp.sum(middle[:, 0], axis=1))
    ref_im = lax.optimization_barrier(jnp.sum(middle[:, 1], axis=1))
    power = lax.optimization_barrier(jnp.sum(middle[:, 0] * middle[:, 0] + middle[:, 1] * middle[:, 1], axis=1))
    scale = 1.0 / jnp.sqrt(power + EPS)

    def one_row(row):
        row_frames = lax.dynamic_index_in_dim(frames, row, 1, keepdims=False)
        row_valid = lax.dynamic_index_in_dim(valid, row, 0, keepdims=False)
        spec = jnp.dot(table, row_frames * row_valid[None, :], preferred_element_type=jnp.float32).reshape(CAV, 2, NB, W)
        real_part = spec[:, 0]
        imag_part = spec[:, 1]
        out_re = (real_part * ref_re[:, None, None] + imag_part * ref_im[:, None, None]) * scale[:, None, None]
        out_im = (imag_part * ref_re[:, None, None] - real_part * ref_im[:, None, None]) * scale[:, None, None]
        return jnp.stack([out_re, out_im], axis=1).astype(jnp.bfloat16)
    rows_out = lax.map(one_row, jnp.arange(ROWS, dtype=jnp.int32))
    return jnp.transpose(rows_out, (1, 2, 3, 0, 4))
```

```python
import functools
import math

import jax
import jax.numpy as jnp
from jax import lax
from jax.experimental import pallas as pl
from jax.experimental.pallas import tpu as pltpu
from jax.sharding import PartitionSpec as P

NB = 128
TWO_PI = 2.0 * math.pi
EPS = 1e-06
LANES = 128
VMEM_LIMIT = 48 * 1024 * 1024


def partner(me, step, n):
    if n & (n - 1) == 0:
        return me ^ step
    return (me + step) % n


def source(me, step, n):
    if n & (n - 1) == 0:
        return me ^ step
    return (me + n - step) % n


def send(value, step, n):
    return lax.ppermute(value, "wave", [(i, partner(i, step, n)) for i in range(n)])


def total_over(value, axis):
    n = lax.axis_size(axis)
    if n & (n - 1):
        return lax.psum(value, axis)
    step = 1
    while step < n:
        value = value + lax.ppermute(value, axis, [(i, i ^ step) for i in range(n)])
        step *= 2
    return value


def prep_kernel(n, rows_dev, chunk, width_all, block_cols, pos_ref, off_ref, cnt_ref, x_ref, pix_ref, *rest):
    outs, picked_ref, wide = rest[:n], rest[n], rest[n + 1]
    frames, rows_all, width = x_ref.shape
    pieces = width // LANES
    for b in range(pieces):
        wide[b] = x_ref[:, :, b * LANES:(b + 1) * LANES].astype(jnp.float32).reshape(
            frames * rows_all, LANES
        )
    me = pos_ref[0]
    first_col = pos_ref[1] + chunk * width
    pix = pix_ref[...]
    total = jnp.zeros((frames, pix.shape[1]), jnp.float32)
    for step in range(n):
        first_row = partner(me, step, n) * rows_dev
        for r in range(rows_dev):
            row = first_row + r
            for b in range(pieces):
                block = (chunk * width + b * LANES) // block_cols
                start = off_ref[block]
                good = (row >= start) & (row < start + cnt_ref[block])
                part = wide[b, pl.ds(row, frames, stride=rows_all), :]
                part = jnp.where(good, part, 0.0)
                outs[step][r, :, b * LANES:(b + 1) * LANES] = part.astype(jnp.bfloat16)
            local = pix - (row * width_all + first_col)
            hot = lax.broadcasted_iota(jnp.int32, (width, pix.shape[1]), 0) == local
            hot = jnp.where(hot, 1.0, 0.0).astype(jnp.bfloat16)
            total += jnp.dot(outs[step][r], hot, preferred_element_type=jnp.float32)
    picked_ref[...] = total


def prep(n, rows_dev, chunk, width, width_all, block_cols, pos, off, cnt, frames, pix):
    frame_dev, rows_all, _ = frames.shape
    npix = pix.shape[1]
    piece = jax.ShapeDtypeStruct((rows_dev, frame_dev, width), jnp.bfloat16)
    return pl.pallas_call(
        functools.partial(prep_kernel, n, rows_dev, chunk, width_all, block_cols),
        out_shape=[piece] * n + [jax.ShapeDtypeStruct((frame_dev, npix), jnp.float32)],
        grid_spec=pltpu.PrefetchScalarGridSpec(
            num_scalar_prefetch=3,
            grid=(1,),
            in_specs=[
                pl.BlockSpec((frame_dev, rows_all, width), lambda i, *_: (0, 0, chunk)),
                pl.BlockSpec((1, npix), lambda i, *_: (0, 0)),
            ],
            out_specs=[pl.BlockSpec(piece.shape, lambda i, *_: (0, 0, 0))] * n
            + [pl.BlockSpec((frame_dev, npix), lambda i, *_: (0, 0))],
            scratch_shapes=[pltpu.VMEM((width // LANES, frame_dev * rows_all, LANES), jnp.float32)],
        ),
        compiler_params=pltpu.CompilerParams(vmem_limit_bytes=VMEM_LIMIT),
        cost_estimate=pl.CostEstimate(flops=1024, bytes_accessed=1024, transcendentals=0),
        name="prep",
    )(pos, off, cnt, frames, pix)


def band_kernel(n, coef_ref, table_ref, *rest):
    pieces, out_ref, flat, mixed = rest[:n], rest[-3], rest[-2], rest[-1]
    rows_dev, frame_dev, width = pieces[0].shape
    nb = table_ref.shape[2]
    cav = pl.program_id(0)

    @pl.when(cav == 0)
    def _():
        for r in range(rows_dev):
            for i in range(n):
                flat[r, i * frame_dev:(i + 1) * frame_dev, :] = pieces[i][r]

    ca = coef_ref[0, cav]
    cb = coef_ref[1, cav]
    for r in range(rows_dev):
        table = table_ref[0].reshape(2 * nb, table_ref.shape[3])
        spec = jnp.dot(table, flat[r], preferred_element_type=jnp.float32)
        re, im = spec[:nb], spec[nb:]
        both = (re * ca + im * cb, im * ca - re * cb)
        for b in range(width // LANES):
            for q in range(2):
                mixed[q, b, pl.ds(r, nb, stride=rows_dev), :] = both[q][:, b * LANES:(b + 1) * LANES]
    for b in range(width // LANES):
        for q in range(2):
            value = mixed[q, b].reshape(nb, rows_dev, LANES).astype(jnp.bfloat16)
            out_ref[0, q, :, :, b * LANES:(b + 1) * LANES] = value


def band(n, chunk, cols_dev, coef, table, pieces, prev):
    rows_dev, frame_dev, width = pieces[0].shape
    ncav, _, nb, frame_total = table.shape
    out = jax.ShapeDtypeStruct((ncav, 2, nb, rows_dev, cols_dev), jnp.bfloat16)
    extra = [] if prev is None else [prev]
    return pl.pallas_call(
        functools.partial(band_kernel, n),
        out_shape=out,
        grid=(ncav,),
        in_specs=[
            pl.BlockSpec(memory_space=pltpu.SMEM),
            pl.BlockSpec((1, 2, nb, frame_total), lambda c: (c, 0, 0, 0)),
        ]
        + [pl.BlockSpec((rows_dev, frame_dev, width), lambda c: (0, 0, 0))] * n
        + [pl.BlockSpec(memory_space=pl.ANY)] * len(extra),
        out_specs=pl.BlockSpec((1, 2, nb, rows_dev, width), lambda c: (c, 0, 0, 0, chunk)),
        scratch_shapes=[
            pltpu.VMEM((rows_dev, frame_total, width), jnp.bfloat16),
            pltpu.VMEM((2, width // LANES, nb * rows_dev, LANES), jnp.float32),
        ],
        input_output_aliases={2 + n: 0} if extra else {},
        compiler_params=pltpu.CompilerParams(vmem_limit_bytes=VMEM_LIMIT),
        cost_estimate=pl.CostEstimate(flops=1024, bytes_accessed=1024, transcendentals=0),
        name="band",
    )(coef, table, *pieces, *extra)


def shards(frames, wavenumbers, band_start, aperture_offset, aperture_count, reference_pixels):
    frame_dev, rows_all, cols_dev = frames.shape
    frame_total = wavenumbers.shape[0]
    n = lax.axis_size("wave")
    me = lax.axis_index("wave")
    rows_dev = rows_all // n
    ncav = band_start.shape[0]
    width_all = cols_dev * lax.axis_size("cols")
    block_cols = cols_dev // aperture_offset.shape[0]
    width = min(256, cols_dev)
    chunks = cols_dev // width
    pos = jnp.stack([me, lax.axis_index("cols") * cols_dev]).astype(jnp.int32)
    pix = reference_pixels[None, :]

    sent, picked = [], 0.0
    for k in range(chunks):
        *parts, part_pick = prep(
            n, rows_dev, k, width, width_all, block_cols, pos, aperture_offset, aperture_count, frames, pix
        )
        sent.append(parts)
        picked = picked + part_pick
        pos, picked = lax.optimization_barrier((pos, picked))

    near = [None] * chunks
    moved = []
    for k in range(chunks):
        parts = sent[k]
        first = parts[1]
        if k >= 1:
            first, _ = lax.optimization_barrier((first, near[k - 1]))
        near[k] = send(first, 1, n)
        far = parts[2:]
        if k >= 2:
            far, _ = lax.optimization_barrier((far, moved[k - 2][2:]))
        moved.append([parts[0], near[k]] + [send(p, 2 + i, n) for i, p in enumerate(far)])

    order = jnp.stack([source(me, s, n) for s in range(n)])
    frame_pos = (order[:, None] * frame_dev + jnp.arange(frame_dev, dtype=jnp.int32)[None, :]).reshape(-1)
    wave_set = jnp.take(wavenumbers.reshape(n, frame_dev), order, axis=0).reshape(-1)
    window = (
        0.5 - 0.5 * jnp.cos(TWO_PI * (frame_pos.astype(jnp.float32) + 0.5) / frame_total)
    ) / math.sqrt(frame_total)
    bins = (band_start[:, None] + jnp.arange(NB, dtype=jnp.int32)[None, :]).astype(jnp.float32)
    angle = bins[:, :, None] * wave_set[None, None, :] * TWO_PI
    table = jnp.stack(
        [jnp.cos(angle) * window, -jnp.sin(angle) * window], axis=1
    ).astype(jnp.bfloat16)

    picked, _ = lax.optimization_barrier((picked, moved[0][2:]))
    middle = table[:, :, NB // 2, :frame_dev].reshape(2 * ncav, frame_dev)
    part = jnp.dot(middle, picked.astype(jnp.bfloat16), preferred_element_type=jnp.float32)
    middle = total_over(total_over(part, "cols"), "wave").reshape(ncav, 2, -1)
    ref = jnp.sum(middle, axis=2)
    power = jnp.sum(middle * middle, axis=(1, 2))
    coef = jnp.transpose(ref / jnp.sqrt(power + EPS)[:, None])

    out = None
    for k in range(chunks):
        out = band(n, k, cols_dev, coef, table, moved[k], out)
    return out


def solution(mesh):
    placed = (
        P("wave", "strips", "cols"),
        P(),
        P(),
        P(("strips", "cols")),
        P(("strips", "cols")),
        P("strips"),
    )
    return jax.shard_map(
        shards,
        mesh=mesh,
        in_specs=placed,
        out_specs=P(None, None, None, ("strips", "wave"), "cols"),
        check_vma=False,
    )
```

```python
import functools
import math

import jax
import jax.numpy as jnp
from jax import lax
from jax.experimental import pallas as pl
from jax.experimental.pallas import tpu as pltpu
from jax.sharding import PartitionSpec as P

NB = 128
TWO_PI = 2.0 * math.pi
EPS = 1e-06
LANES = 128
VMEM_LIMIT = 48 * 1024 * 1024


def partner(me, step, n):
    if n & (n - 1) == 0:
        return me ^ step
    return (me + step) % n


def source(me, step, n):
    if n & (n - 1) == 0:
        return me ^ step
    return (me + n - step) % n


def column_cuts(cols_dev):
    if cols_dev % 256 or cols_dev < 512:
        return [(LANES, i) for i in range(cols_dev // LANES)]
    return [(128, 0)] + [(256, i) for i in range(1, cols_dev // 256)] + [(128, 1)]


def send(value, step, n):
    return lax.ppermute(value, "wave", [(i, partner(i, step, n)) for i in range(n)])


def total_over(value, axis):
    n = lax.axis_size(axis)
    if n & (n - 1):
        return lax.psum(value, axis)
    step = 1
    while step < n:
        value = value + lax.ppermute(value, axis, [(i, i ^ step) for i in range(n)])
        step *= 2
    return value


def prep_kernel(n, rows_dev, chunk, width_all, block_cols, pos_ref, off_ref, cnt_ref, x_ref, pix_ref, *rest):
    outs, picked_ref, wide = rest[:n], rest[n], rest[n + 1]
    frames, rows_all, width = x_ref.shape
    pieces = width // LANES
    for b in range(pieces):
        wide[b] = x_ref[:, :, b * LANES:(b + 1) * LANES].astype(jnp.float32).reshape(
            frames * rows_all, LANES
        )
    me = pos_ref[0]
    first_col = pos_ref[1] + chunk * width
    pix = pix_ref[...]
    total = jnp.zeros((frames, pix.shape[1]), jnp.float32)
    for step in range(n):
        first_row = partner(me, step, n) * rows_dev
        for r in range(rows_dev):
            row = first_row + r
            for b in range(pieces):
                block = (chunk * width + b * LANES) // block_cols
                start = off_ref[block]
                good = (row >= start) & (row < start + cnt_ref[block])
                part = wide[b, pl.ds(row, frames, stride=rows_all), :]
                part = jnp.where(good, part, 0.0)
                outs[step][r, :, b * LANES:(b + 1) * LANES] = part.astype(jnp.bfloat16)
            local = pix - (row * width_all + first_col)
            hot = lax.broadcasted_iota(jnp.int32, (width, pix.shape[1]), 0) == local
            hot = jnp.where(hot, 1.0, 0.0).astype(jnp.bfloat16)
            total += jnp.dot(outs[step][r], hot, preferred_element_type=jnp.float32)
    picked_ref[...] = total


def prep(n, rows_dev, chunk, width, width_all, block_cols, pos, off, cnt, frames, pix):
    frame_dev, rows_all, _ = frames.shape
    npix = pix.shape[1]
    piece = jax.ShapeDtypeStruct((rows_dev, frame_dev, width), jnp.bfloat16)
    return pl.pallas_call(
        functools.partial(prep_kernel, n, rows_dev, chunk, width_all, block_cols),
        out_shape=[piece] * n + [jax.ShapeDtypeStruct((frame_dev, npix), jnp.float32)],
        grid_spec=pltpu.PrefetchScalarGridSpec(
            num_scalar_prefetch=3,
            grid=(1,),
            in_specs=[
                pl.BlockSpec((frame_dev, rows_all, width), lambda i, *_: (0, 0, chunk)),
                pl.BlockSpec((1, npix), lambda i, *_: (0, 0)),
            ],
            out_specs=[pl.BlockSpec(piece.shape, lambda i, *_: (0, 0, 0))] * n
            + [pl.BlockSpec((frame_dev, npix), lambda i, *_: (0, 0))],
            scratch_shapes=[pltpu.VMEM((width // LANES, frame_dev * rows_all, LANES), jnp.float32)],
        ),
        compiler_params=pltpu.CompilerParams(vmem_limit_bytes=VMEM_LIMIT),
        cost_estimate=pl.CostEstimate(flops=1024, bytes_accessed=1024, transcendentals=0),
        name="prep",
    )(pos, off, cnt, frames, pix)


def band_kernel(n, coef_ref, table_ref, *rest):
    pieces, out_ref, flat, mixed = rest[:n], rest[-3], rest[-2], rest[-1]
    rows_dev, frame_dev, width = pieces[0].shape
    nb = table_ref.shape[2]
    cav = pl.program_id(0)

    @pl.when(cav == 0)
    def _():
        for r in range(rows_dev):
            for i in range(n):
                flat[i * frame_dev:(i + 1) * frame_dev, r * width:(r + 1) * width] = pieces[i][r]

    ca = coef_ref[0, cav]
    cb = coef_ref[1, cav]
    table = table_ref[0].reshape(2 * nb, table_ref.shape[3])
    group = min(rows_dev, max(1, 256 // width))
    for g in range(0, rows_dev, group):
        spec = jnp.dot(
            table, flat[:, g * width:(g + group) * width], preferred_element_type=jnp.float32
        )
        re, im = spec[:nb], spec[nb:]
        both = (re * ca + im * cb, im * ca - re * cb)
        for r in range(group):
            for b in range(width // LANES):
                first = r * width + b * LANES
                for q in range(2):
                    mixed[q, b, pl.ds(g + r, nb, stride=rows_dev), :] = both[q][:, first:first + LANES]
    for b in range(width // LANES):
        for q in range(2):
            value = mixed[q, b].reshape(nb, rows_dev, LANES).astype(jnp.bfloat16)
            out_ref[0, q, :, :, b * LANES:(b + 1) * LANES] = value


def band(n, chunk, cols_dev, coef, table, pieces, prev):
    rows_dev, frame_dev, width = pieces[0].shape
    ncav, _, nb, frame_total = table.shape
    out = jax.ShapeDtypeStruct((ncav, 2, nb, rows_dev, cols_dev), jnp.bfloat16)
    extra = [] if prev is None else [prev]
    return pl.pallas_call(
        functools.partial(band_kernel, n),
        out_shape=out,
        grid=(ncav,),
        in_specs=[
            pl.BlockSpec(memory_space=pltpu.SMEM),
            pl.BlockSpec((1, 2, nb, frame_total), lambda c: (c, 0, 0, 0)),
        ]
        + [pl.BlockSpec((rows_dev, frame_dev, width), lambda c: (0, 0, 0))] * n
        + [pl.BlockSpec(memory_space=pl.ANY)] * len(extra),
        out_specs=pl.BlockSpec((1, 2, nb, rows_dev, width), lambda c: (c, 0, 0, 0, chunk)),
        scratch_shapes=[
            pltpu.VMEM((frame_total, rows_dev * width), jnp.bfloat16),
            pltpu.VMEM((2, width // LANES, nb * rows_dev, LANES), jnp.float32),
        ],
        input_output_aliases={2 + n: 0} if extra else {},
        compiler_params=pltpu.CompilerParams(vmem_limit_bytes=VMEM_LIMIT),
        cost_estimate=pl.CostEstimate(flops=1024, bytes_accessed=1024, transcendentals=0),
        name="band",
    )(coef, table, *pieces, *extra)


def shards(frames, wavenumbers, band_start, aperture_offset, aperture_count, reference_pixels):
    frame_dev, rows_all, cols_dev = frames.shape
    frame_total = wavenumbers.shape[0]
    n = lax.axis_size("wave")
    me = lax.axis_index("wave")
    rows_dev = rows_all // n
    ncav = band_start.shape[0]
    width_all = cols_dev * lax.axis_size("cols")
    block_cols = cols_dev // aperture_offset.shape[0]
    cuts = column_cuts(cols_dev)
    chunks = len(cuts)
    pos = jnp.stack([me, lax.axis_index("cols") * cols_dev]).astype(jnp.int32)
    pix = reference_pixels[None, :]

    sent, picked = [], 0.0
    for width, index in cuts:
        *parts, part_pick = prep(
            n, rows_dev, index, width, width_all, block_cols, pos, aperture_offset, aperture_count, frames, pix
        )
        sent.append(parts)
        picked = picked + part_pick
        pos, picked = lax.optimization_barrier((pos, picked))

    near = [None] * chunks
    moved = []
    for k in range(chunks):
        parts = sent[k]
        first = parts[1]
        if k >= 1:
            first, _ = lax.optimization_barrier((first, near[k - 1]))
        near[k] = send(first, 1, n)
        far = parts[2:]
        if k >= 2:
            far = [lax.optimization_barrier((p, q))[0] for p, q in zip(far, moved[k - 2][2:])]
        moved.append([parts[0], near[k]] + [send(p, 2 + i, n) for i, p in enumerate(far)])

    order = jnp.stack([source(me, s, n) for s in range(n)])
    frame_pos = (order[:, None] * frame_dev + jnp.arange(frame_dev, dtype=jnp.int32)[None, :]).reshape(-1)
    wave_set = jnp.take(wavenumbers.reshape(n, frame_dev), order, axis=0).reshape(-1)
    window = (
        0.5 - 0.5 * jnp.cos(TWO_PI * (frame_pos.astype(jnp.float32) + 0.5) / frame_total)
    ) / math.sqrt(frame_total)
    bins = (band_start[:, None] + jnp.arange(NB, dtype=jnp.int32)[None, :]).astype(jnp.float32)
    angle = bins[:, :, None] * wave_set[None, None, :] * TWO_PI
    table = jnp.stack(
        [jnp.cos(angle) * window, -jnp.sin(angle) * window], axis=1
    ).astype(jnp.bfloat16)

    picked, _ = lax.optimization_barrier((picked, moved[min(1, chunks - 1)][2:]))
    middle = table[:, :, NB // 2, :frame_dev].reshape(2 * ncav, frame_dev)
    part = jnp.dot(middle, picked.astype(jnp.bfloat16), preferred_element_type=jnp.float32)
    middle = total_over(total_over(part, "cols"), "wave").reshape(ncav, 2, -1)
    ref = jnp.sum(middle, axis=2)
    power = jnp.sum(middle * middle, axis=(1, 2))
    coef = jnp.transpose(ref / jnp.sqrt(power + EPS)[:, None])

    out = None
    for k in range(chunks):
        out = band(n, cuts[k][1], cols_dev, coef, table, moved[k], out)
    return out


def solution(mesh):
    placed = (
        P("wave", "strips", "cols"),
        P(),
        P(),
        P(("strips", "cols")),
        P(("strips", "cols")),
        P("strips"),
    )
    return jax.shard_map(
        shards,
        mesh=mesh,
        in_specs=placed,
        out_specs=P(None, None, None, ("strips", "wave"), "cols"),
        check_vma=False,
    )
```

```python
import functools
import math

import jax
import jax.numpy as jnp
from jax import lax
from jax.experimental import pallas as pl
from jax.experimental.pallas import tpu as pltpu
from jax.sharding import PartitionSpec as P

NB = 128
TWO_PI = 2.0 * math.pi
EPS = 1e-06
LANES = 128
VMEM_LIMIT = 48 * 1024 * 1024


def partner(me, step, n):
    if n & (n - 1) == 0:
        return me ^ step
    return (me + step) % n


def source(me, step, n):
    if n & (n - 1) == 0:
        return me ^ step
    return (me + n - step) % n


def column_cuts(cols_dev):
    if cols_dev % 256 or cols_dev < 512:
        return [(LANES, i) for i in range(cols_dev // LANES)]
    return [(128, 0)] + [(256, i) for i in range(1, cols_dev // 256)] + [(128, 1)]


def send(value, step, n):
    return lax.ppermute(value, "wave", [(i, partner(i, step, n)) for i in range(n)])


def total_over(value, axis):
    n = lax.axis_size(axis)
    if n & (n - 1):
        return lax.psum(value, axis)
    step = 1
    while step < n:
        value = value + lax.ppermute(value, axis, [(i, i ^ step) for i in range(n)])
        step *= 2
    return value


def prep_kernel(n, rows_dev, chunk, width_all, block_cols, pos_ref, off_ref, cnt_ref, x_ref, pix_ref, *rest):
    outs, picked_ref, wide = rest[:n], rest[n], rest[n + 1]
    frames, rows_all, width = x_ref.shape
    pieces = width // LANES
    for b in range(pieces):
        wide[b] = x_ref[:, :, b * LANES:(b + 1) * LANES].astype(jnp.float32).reshape(
            frames * rows_all, LANES
        )
    me = pos_ref[0]
    first_col = pos_ref[1] + chunk * width
    pix = pix_ref[...]
    total = jnp.zeros((frames, pix.shape[1]), jnp.float32)
    for step in range(n):
        first_row = partner(me, step, n) * rows_dev
        for r in range(rows_dev):
            row = first_row + r
            for b in range(pieces):
                block = (chunk * width + b * LANES) // block_cols
                start = off_ref[block]
                good = (row >= start) & (row < start + cnt_ref[block])
                part = wide[b, pl.ds(row, frames, stride=rows_all), :]
                part = jnp.where(good, part, 0.0)
                outs[step][r, :, b * LANES:(b + 1) * LANES] = part.astype(jnp.bfloat16)
            local = pix - (row * width_all + first_col)
            hot = lax.broadcasted_iota(jnp.int32, (width, pix.shape[1]), 0) == local
            hot = jnp.where(hot, 1.0, 0.0).astype(jnp.bfloat16)
            total += jnp.dot(outs[step][r], hot, preferred_element_type=jnp.float32)
    picked_ref[...] = total


def prep(n, rows_dev, chunk, width, width_all, block_cols, pos, off, cnt, frames, pix):
    frame_dev, rows_all, _ = frames.shape
    npix = pix.shape[1]
    piece = jax.ShapeDtypeStruct((rows_dev, frame_dev, width), jnp.bfloat16)
    return pl.pallas_call(
        functools.partial(prep_kernel, n, rows_dev, chunk, width_all, block_cols),
        out_shape=[piece] * n + [jax.ShapeDtypeStruct((frame_dev, npix), jnp.float32)],
        grid_spec=pltpu.PrefetchScalarGridSpec(
            num_scalar_prefetch=3,
            grid=(1,),
            in_specs=[
                pl.BlockSpec((frame_dev, rows_all, width), lambda i, *_: (0, 0, chunk)),
                pl.BlockSpec((1, npix), lambda i, *_: (0, 0)),
            ],
            out_specs=[pl.BlockSpec(piece.shape, lambda i, *_: (0, 0, 0))] * n
            + [pl.BlockSpec((frame_dev, npix), lambda i, *_: (0, 0))],
            scratch_shapes=[pltpu.VMEM((width // LANES, frame_dev * rows_all, LANES), jnp.float32)],
        ),
        compiler_params=pltpu.CompilerParams(vmem_limit_bytes=VMEM_LIMIT),
        cost_estimate=pl.CostEstimate(flops=1024, bytes_accessed=1024, transcendentals=0),
        name="prep",
    )(pos, off, cnt, frames, pix)


def band_kernel(n, coef_ref, table_ref, *rest):
    pieces, out_ref, flat, mixed = rest[:n], rest[-3], rest[-2], rest[-1]
    rows_dev, frame_dev, width = pieces[0].shape
    nb = table_ref.shape[2]
    cav = pl.program_id(0)

    @pl.when(cav == 0)
    def _():
        for r in range(rows_dev):
            for i in range(n):
                flat[i * frame_dev:(i + 1) * frame_dev, r * width:(r + 1) * width] = pieces[i][r]

    ca = coef_ref[0, cav]
    cb = coef_ref[1, cav]
    table = table_ref[0].reshape(2 * nb, table_ref.shape[3])
    group = min(rows_dev, max(1, 256 // width))
    for g in range(0, rows_dev, group):
        spec = jnp.dot(
            table, flat[:, g * width:(g + group) * width], preferred_element_type=jnp.float32
        )
        re, im = spec[:nb], spec[nb:]
        both = (re * ca + im * cb, im * ca - re * cb)
        for r in range(group):
            for b in range(width // LANES):
                first = r * width + b * LANES
                for q in range(2):
                    mixed[q, b, pl.ds(g + r, nb, stride=rows_dev), :] = both[q][:, first:first + LANES]
    for b in range(width // LANES):
        for q in range(2):
            value = mixed[q, b].reshape(nb, rows_dev, LANES).astype(jnp.bfloat16)
            out_ref[0, q, :, :, b * LANES:(b + 1) * LANES] = value


def band(n, chunk, cols_dev, coef, table, pieces, prev):
    rows_dev, frame_dev, width = pieces[0].shape
    ncav, _, nb, frame_total = table.shape
    out = jax.ShapeDtypeStruct((ncav, 2, nb, rows_dev, cols_dev), jnp.bfloat16)
    extra = [] if prev is None else [prev]
    return pl.pallas_call(
        functools.partial(band_kernel, n),
        out_shape=out,
        grid=(ncav,),
        in_specs=[
            pl.BlockSpec(memory_space=pltpu.SMEM),
            pl.BlockSpec((1, 2, nb, frame_total), lambda c: (c, 0, 0, 0)),
        ]
        + [pl.BlockSpec((rows_dev, frame_dev, width), lambda c: (0, 0, 0))] * n
        + [pl.BlockSpec(memory_space=pl.ANY)] * len(extra),
        out_specs=pl.BlockSpec((1, 2, nb, rows_dev, width), lambda c: (c, 0, 0, 0, chunk)),
        scratch_shapes=[
            pltpu.VMEM((frame_total, rows_dev * width), jnp.bfloat16),
            pltpu.VMEM((2, width // LANES, nb * rows_dev, LANES), jnp.float32),
        ],
        input_output_aliases={2 + n: 0} if extra else {},
        compiler_params=pltpu.CompilerParams(vmem_limit_bytes=VMEM_LIMIT),
        cost_estimate=pl.CostEstimate(flops=1024, bytes_accessed=1024, transcendentals=0),
        name="band",
    )(coef, table, *pieces, *extra)


def shards(frames, wavenumbers, band_start, aperture_offset, aperture_count, reference_pixels):
    frame_dev, rows_all, cols_dev = frames.shape
    frame_total = wavenumbers.shape[0]
    n = lax.axis_size("wave")
    me = lax.axis_index("wave")
    rows_dev = rows_all // n
    ncav = band_start.shape[0]
    width_all = cols_dev * lax.axis_size("cols")
    block_cols = cols_dev // aperture_offset.shape[0]
    cuts = column_cuts(cols_dev)
    chunks = len(cuts)
    pos = jnp.stack([me, lax.axis_index("cols") * cols_dev]).astype(jnp.int32)
    pix = reference_pixels[None, :]

    sent, picked = [], 0.0
    for width, index in cuts:
        *parts, part_pick = prep(
            n, rows_dev, index, width, width_all, block_cols, pos, aperture_offset, aperture_count, frames, pix
        )
        sent.append(parts)
        picked = picked + part_pick
        pos, picked = lax.optimization_barrier((pos, picked))

    near = [None] * chunks
    moved = []
    for k in range(chunks):
        parts = sent[k]
        first = parts[1]
        if k >= 1:
            first, _ = lax.optimization_barrier((first, near[k - 1]))
        near[k] = send(first, 1, n)
        far = parts[2:]
        if k >= 2:
            far = [lax.optimization_barrier((p, q))[0] for p, q in zip(far, moved[k - 2][2:])]
        moved.append([parts[0], near[k]] + [send(p, 2 + i, n) for i, p in enumerate(far)])

    (wavenumbers, band_start), _ = lax.optimization_barrier(((wavenumbers, band_start), moved[0][2:]))
    order = jnp.stack([source(me, s, n) for s in range(n)])
    frame_pos = (order[:, None] * frame_dev + jnp.arange(frame_dev, dtype=jnp.int32)[None, :]).reshape(-1)
    wave_set = jnp.take(wavenumbers.reshape(n, frame_dev), order, axis=0).reshape(-1)
    window = (
        0.5 - 0.5 * jnp.cos(TWO_PI * (frame_pos.astype(jnp.float32) + 0.5) / frame_total)
    ) / math.sqrt(frame_total)
    bins = (band_start[:, None] + jnp.arange(NB, dtype=jnp.int32)[None, :]).astype(jnp.float32)
    angle = bins[:, :, None] * wave_set[None, None, :] * TWO_PI
    table = jnp.stack(
        [jnp.cos(angle) * window, -jnp.sin(angle) * window], axis=1
    ).astype(jnp.bfloat16)

    own = bins[:, NB // 2, None] * wave_set[None, :frame_dev] * TWO_PI
    (own, picked), _ = lax.optimization_barrier(((own, picked), moved[min(1, chunks - 1)][2:]))
    middle = jnp.stack(
        [jnp.cos(own) * window[:frame_dev], -jnp.sin(own) * window[:frame_dev]], axis=1
    ).astype(jnp.bfloat16).reshape(2 * ncav, frame_dev)
    part = jnp.dot(middle, picked.astype(jnp.bfloat16), preferred_element_type=jnp.float32)
    middle = total_over(total_over(part, "cols"), "wave").reshape(ncav, 2, -1)
    ref = jnp.sum(middle, axis=2)
    power = jnp.sum(middle * middle, axis=(1, 2))
    coef = jnp.transpose(ref / jnp.sqrt(power + EPS)[:, None])

    out = None
    for k in range(chunks):
        out = band(n, cuts[k][1], cols_dev, coef, table, moved[k], out)
    return out


def solution(mesh):
    placed = (
        P("wave", "strips", "cols"),
        P(),
        P(),
        P(("strips", "cols")),
        P(("strips", "cols")),
        P("strips"),
    )
    return jax.shard_map(
        shards,
        mesh=mesh,
        in_specs=placed,
        out_specs=P(None, None, None, ("strips", "wave"), "cols"),
        check_vma=False,
    )
```
